32 devices in a mesh: grp: 4 (over z), list: 8 (over y, x, core).
Axes of the slice: x: 2, y: 2, z: 4, core: 2. Of those that a mesh axis runs over, the one named last changes fastest.
Arguments:
- vectors: bfloat16 [3, 16384, 1024], P(None, ('grp', 'list')), may hold values from -6 to 6
- owner_route: int32 [3, 16384, 1], P(None, ('grp', 'list')), may hold values from 0 to 7; in each aligned block of 512 rows (0 to 511, 512 to 1023, ..., all dimensions but the last counted through in order) at most 128 rows name the same one
- list_slot: int32 [3, 16384], P(None, ('grp', 'list')), may hold values from 0 to 1023
- centroids: float32 [8192, 1024], P('list'), may hold values from -6 to 6
- counts: int32 [8192], P('list'), may hold values from 1 to 8
Outputs:
- residuals: bfloat16 [3, 16384, 1024], P(None, ('grp', 'list'))
- new_centroids: float32 [8192, 1024], P('list')
The draws below stay inside these ranges and needn't reach their ends.
Inputs may be any that keep to these rules, and one draw needn't show every extreme that they name: `owner_route`: within the rows of one device for one step, at most 128 vectors name the same owner; some owner is named exactly 128 times.
All inputs are finite; a program needn't handle non-finite values.
Results may differ from the reference program's by a relative error of at most 0.0035.
Values may be sent and summed in bfloat16 or wider, within the bound.
A program may use at most 128 MiB of HBM per device.

```python
import math
import jax
import jax.numpy as jnp
import numpy as np

D = 1024
LIST_DEV = 1024
ROWS = 512
STEPS = 3
OWNERS = 8
CAP = 128
LISTS = 8192
VECS = 16384


def set_ends(entries, key, smallest, largest):
    index_at = [jax.random.randint(jax.random.fold_in(key, axis), (), 0, length) for axis, length in enumerate(entries.shape)]
    widest = entries.shape.index(max(entries.shape))
    next_to = index_at[:widest] + [(index_at[widest] + 1) % entries.shape[widest]] + index_at[widest + 1:]
    return entries.at[tuple(index_at)].set(smallest).at[tuple(next_to)].set(largest)


def steps_of(stream_key, extent, shards, low, largest):
    loudness = 1.0
    for dim, blocks in shards:
        draws = jax.random.uniform(jax.random.fold_in(jax.random.fold_in(stream_key, 6), dim), (blocks,), jnp.float32, low / len(shards), largest / len(shards))
        loudness = loudness * jnp.repeat(jnp.exp(draws), extent[dim] // blocks).reshape((-1,) + (1,) * (len(extent) - 1 - dim))
    return loudness


def deal_out(key, own, number, rows, number_of, top, most, lean):
    sequence = jax.random.permutation(key, number_of)
    crowded, ordinary = shares(number_of, rows * top, most, lean, True), shares(number_of, rows * top, most, lean, False)
    places = jnp.arange(number_of)

    def named(tallies, turn):
        used = int((tallies > 0).sum())
        fixed = max(1, used // 4)
        shifted = fixed + (places - fixed + turn * (used - fixed)) % max(1, number_of - fixed)
        return jnp.zeros((number_of,), jnp.int32).at[sequence[jnp.where(places < fixed, places, shifted)]].set(jnp.asarray(tallies, jnp.int32))

    tallies = jnp.where(number % 4 == 0, named(crowded, number // 4), named(ordinary, number - number // 4 - 1))
    mixed = jax.random.permutation(jax.random.fold_in(own, 3), number_of)
    giver, sink = mixed[0:number_of // 2 * 2:2], mixed[1:number_of // 2 * 2:2]
    room = jnp.minimum(tallies[giver] - 1, most - tallies[sink]) // 2
    room = jnp.where((giver == sequence[0]) | (sink == sequence[0]) | (tallies[sink] == 0), 0, jnp.maximum(room, 0))
    shifted = jax.random.randint(jax.random.fold_in(own, 4), (number_of // 2,), 0, 1 << 20) % (room + 1)
    tallies = tallies.at[giver].add(-shifted).at[sink].add(shifted)
    items = jnp.searchsorted(jnp.cumsum(tallies), jnp.arange(rows * top), side="right").astype(jnp.int32)
    listing = items.reshape(top, rows).T
    listing = listing[jax.random.permutation(jax.random.fold_in(own, 1), rows)]
    turn = jax.random.randint(jax.random.fold_in(own, 2), (rows, 1), 0, top)
    return jnp.take_along_axis(listing, (jnp.arange(top)[None, :] + turn) % top, axis=1)


def shares(amount, total, bound, lean, full):
    portions = [(1 << 20) // math.isqrt(standing ** lean) + 1 for standing in range(1, amount + 1)]
    largest = bound if full else min(bound, max(-(-total // amount), total * portions[0] // sum(portions)))
    least = 1 if total - largest >= amount - 1 else 0
    given, surplus = [largest] + [least] * (amount - 1), total - largest - least * (amount - 1)
    while surplus > 0:
        candidates = [i for i in range(1, amount) if given[i] < largest] or [i for i in range(1, amount) if given[i] < bound]
        whole, remaining = sum([portions[i] for i in candidates]), surplus
        for i in candidates:
            more = min(bound - given[i], max(1, remaining * portions[i] // whole), surplus)
            given[i] = given[i] + more
            surplus = surplus - more
    return np.array(given)


def bell_draw(rng, dims, spread, limit, split=(), held_as=jnp.bfloat16):
    array = jax.random.normal(rng, dims, jnp.float32) * spread
    if len(split) > 0:
        array = steps_of(rng, dims, split, -0.22, 0.18) * array
    return jnp.clip(array, min=-limit, max=limit).astype(held_as)


def setup_inputs(seed: int = 0) -> dict:
    streams_of = jax.random.split(jax.random.key(seed), 6)
    vectors = bell_draw(streams_of[0], (STEPS, VECS, D), 1.0, 6.0, ((1, 32),))
    owner_route_keys = jax.random.split(jax.random.fold_in(streams_of[1], 1), STEPS * VECS // ROWS)
    owner_route_turns = jax.random.permutation(jax.random.fold_in(streams_of[1], 3), STEPS * VECS // ROWS)
    owner_route = jax.vmap(lambda own, number: deal_out(jax.random.fold_in(streams_of[1], 2), own, number, ROWS, OWNERS, 1, CAP, 2))(owner_route_keys, owner_route_turns).reshape((STEPS, VECS, 1))
    list_slot = set_ends(jax.random.randint(streams_of[2], (STEPS, VECS), 0, LIST_DEV), jax.random.fold_in(streams_of[2], 1), 0, LIST_DEV - 1).astype(jnp.int32)
    centroids = bell_draw(streams_of[3], (LISTS, D), 1.0, 6.0, ((0, 8),), jnp.float32)
    counts = set_ends(jax.random.randint(streams_of[4], (LISTS,), 1, 9), jax.random.fold_in(streams_of[4], 1), 1, 8).astype(jnp.int32)
    return {"vectors": vectors, "owner_route": owner_route, "list_slot": list_slot, "centroids": centroids, "counts": counts}


def reference(vectors, owner_route, list_slot, centroids, counts):
    current = centroids
    weights = counts.astype(jnp.float32)
    outputs = []
    for step_index in range(STEPS):
        list_ids = (owner_route[step_index, :, 0] * LIST_DEV + list_slot[step_index]).astype(jnp.int32)
        vec_float = vectors[step_index].astype(jnp.float32)
        residual_rows = (vec_float - current[list_ids]).astype(jnp.bfloat16)
        outputs.append(residual_rows)
        sums = jax.ops.segment_sum(vec_float, list_ids, num_segments=LISTS)
        batch_count = jax.ops.segment_sum(jnp.ones((vec_float.shape[0],), jnp.float32), list_ids, num_segments=LISTS)
        current = (weights[:, None] * current + sums) / (weights + batch_count)[:, None]
        weights = weights + batch_count
    return jnp.stack(outputs, axis=0), current
```

```python
import functools

import jax
import jax.numpy as jnp
from jax import lax
from jax.experimental import pallas as pl
from jax.experimental.pallas import tpu as pltpu
from jax.sharding import PartitionSpec as P

MESH = pl.DeviceIdType.MESH
BF16 = jnp.bfloat16
F32 = jnp.float32
I32 = jnp.int32


def one_hot(mask):
    return jnp.where(mask, 1.0, 0.0).astype(BF16)


def dot(a, b):
    return jnp.dot(a, b, preferred_element_type=F32)


def loop(count, body):
    def step(i, carry):
        body(i)
        return carry

    lax.fori_loop(0, count, step, 0)


def rows_at(start, size):
    return pl.ds(pl.multiple_of(start, size), size)


def kernel(
    dims,
    vec_hbm, owner_ref, slot_ref, cent_hbm, counts_ref,
    out_hbm, new_hbm,
    vec, send, recv, back, part, from_left, from_right, num, high, low,
    send_slots, recv_slots, slot_row, slot_col, dest_row, dest_col, count_col, count_msg, weight_col,
    load_sem, out_sem, slot_send, slot_recv, disp_send, disp_recv, ret_send, ret_recv,
    right_send, left_send, left_recv, right_recv, cnt_send, cnt_recv,
):
    steps, rows, width, owners, groups, lists, cap = dims
    places = owners * cap
    quarter = lists // groups
    pack = 128 // cap
    me = lax.axis_index("list")
    z = lax.axis_index("grp")

    loads = [pltpu.make_async_copy(vec_hbm.at[s], vec.at[s], load_sem.at[s]) for s in range(steps)]
    loads.append(pltpu.make_async_copy(cent_hbm, num, load_sem.at[steps]))
    for load in loads:
        load.start()

    barrier = pltpu.get_barrier_semaphore()

    def greet_owner(i):
        pl.semaphore_signal(barrier, inc=1, device_id={"list": lax.rem(me + i + 1, owners)}, device_id_type=MESH)

    def greet_group(i):
        pl.semaphore_signal(barrier, inc=1, device_id={"grp": lax.rem(z + i + 1, groups)}, device_id_type=MESH)

    loop(owners - 1, greet_owner)
    loop(groups - 1, greet_group)

    owner_iota = lax.broadcasted_iota(I32, (owners, rows), 0)
    before = one_hot(
        lax.broadcasted_iota(I32, (rows, rows), 0) < lax.broadcasted_iota(I32, (rows, rows), 1)
    )
    hits, ranks, dests = [], [], []
    for s in range(steps):
        hit = jnp.where(owner_iota == owner_ref[s : s + 1, :], 1.0, 0.0)
        rank = hit * dot(hit.astype(BF16), before)
        hits.append(hit)
        ranks.append(jnp.sum(rank, axis=0, keepdims=True))
        dests.append(jnp.sum(rank + hit * (owner_iota * cap).astype(F32), axis=0, keepdims=True))
        dest_row[s : s + 1, :] = dests[s].astype(I32)
    table = jnp.concatenate(dests + ranks + [jnp.zeros((128 - 2 * steps, rows), F32)], axis=0)
    dest_col[...] = jnp.transpose(table).astype(I32)

    send_slots[...] = jnp.zeros_like(send_slots)
    lane = lax.broadcasted_iota(I32, (rows, 128), 1)
    for s in range(steps):
        value = slot_ref[s : s + 1, :] + 1
        upper = (value // 32).astype(F32)
        lower = (value % 32).astype(F32)
        spot = one_hot(lane == dest_col[:, steps + s : steps + s + 1] + lax.rem(me, pack) * cap)
        line = 32.0 * dot((hits[s] * upper).astype(BF16), spot) + dot((hits[s] * lower).astype(BF16), spot)
        for p in range(owners):
            send_slots[p, s : s + 1, :] = line[p : p + 1, :]
    recv_slots[me] = send_slots[me]

    pl.semaphore_wait(barrier, owners - 1 + groups - 1)

    def send_slot(i):
        p = lax.rem(me + i + 1, owners)
        pltpu.make_async_remote_copy(
            src_ref=send_slots.at[p], dst_ref=recv_slots.at[me], send_sem=slot_send, recv_sem=slot_recv,
            device_id={"list": p}, device_id_type=MESH,
        ).start()

    loop(owners - 1, send_slot)

    tile = min(256, places)

    def pack_rows(s):
        loads[s].wait()

        def body(i):
            at = rows_at(i * tile, tile)
            place = lax.broadcasted_iota(I32, (tile, rows), 0) + i * tile
            send[s, at, :] = dot(one_hot(place == dest_row[s : s + 1, :]), vec[s]).astype(BF16)

        loop(places // tile, body)
        mine = rows_at(me * cap, cap)
        recv[s, mine, :] = send[s, mine, :]

    def exchange(src, dst, s, send_sem, recv_sem):
        def body(i):
            p = lax.rem(me + i + 1, owners)
            pltpu.make_async_remote_copy(
                src_ref=src.at[s, rows_at(p * cap, cap)], dst_ref=dst.at[s, rows_at(me * cap, cap)],
                send_sem=send_sem.at[s], recv_sem=recv_sem.at[s],
                device_id={"list": p}, device_id_type=MESH,
            ).start()

        loop(owners - 1, body)

    def drain(ref, s, sem):
        others = ref.at[s, pl.ds(0, (owners - 1) * cap)]
        pltpu.make_async_copy(others, others, sem.at[s]).wait()

    def split_table():
        def body(i):
            at = rows_at(i * quarter, quarter)
            value = num[at, :]
            top = value.astype(BF16)
            high[at, :] = top
            low[at, :] = (value - top.astype(F32)).astype(BF16)

        loop(groups, body)

    def get_slots():
        others = recv_slots.at[pl.ds(0, owners - 1)]
        pltpu.make_async_copy(others, others, slot_recv).wait()
        chunks = []
        for c in range(owners // pack):
            chunk = recv_slots[c * pack]
            for i in range(1, pack):
                chunk = chunk + recv_slots[c * pack + i]
            chunks.append(chunk)
        line = jnp.concatenate(chunks, axis=1) - 1.0
        slot_row[...] = line.astype(I32)
        tall = jnp.concatenate([line, jnp.zeros((120, places), F32)], axis=0)
        slot_col[...] = jnp.transpose(tall).astype(I32)
        count_col[...] = jnp.zeros_like(count_col)

    def list_sums(s):
        def body(i):
            at = rows_at(i * quarter, quarter)
            name = lax.broadcasted_iota(I32, (quarter, places), 0) + i * quarter
            mask = jnp.where(name == slot_row[s : s + 1, :], 1.0, 0.0)
            part[s, i] = dot(mask.astype(BF16), recv[s]).astype(BF16)
            column = lax.broadcasted_iota(I32, (quarter, 128), 1)
            count_col[at, :] = jnp.where(column == s, jnp.sum(mask, axis=1, keepdims=True), count_col[at, :])

        loop(groups, body)

    def residual(s):
        def body(i):
            at = rows_at(i * tile, tile)
            pick = one_hot(lax.broadcasted_iota(I32, (tile, lists), 1) == slot_col[at, s : s + 1])
            chosen = dot(pick, high[...]) + dot(pick, low[...])
            recv[s, at, :] = (recv[s, at, :].astype(F32) - chosen).astype(BF16)

        loop(places // tile, body)
        mine = rows_at(me * cap, cap)
        back[s, mine, :] = recv[s, mine, :]
        exchange(recv, back, s, ret_send, ret_recv)

    out_tile = min(256, rows)

    def unpack_rows(s):
        drain(back, s, ret_recv)

        def body(i):
            at = rows_at(i * out_tile, out_tile)
            pick = one_hot(lax.broadcasted_iota(I32, (out_tile, places), 1) == dest_col[at, s : s + 1])
            vec[s, at, :] = dot(pick, back[s]).astype(BF16)

        loop(rows // out_tile, body)
        pltpu.make_async_copy(vec.at[s], out_hbm.at[s], out_sem.at[s]).start()

    def send_counts():
        count_msg[z] = jnp.transpose(count_col[...])[0:8, :]

        def body(i):
            g = lax.rem(z + i + 1, groups)
            pltpu.make_async_remote_copy(
                src_ref=count_msg.at[z], dst_ref=count_msg.at[z], send_sem=cnt_send, recv_sem=cnt_recv,
                device_id={"grp": g}, device_id_type=MESH,
            ).start()

        loop(groups - 1, body)

    def get_counts():
        others = count_msg.at[pl.ds(0, groups - 1)]
        pltpu.make_async_copy(others, others, cnt_recv).wait()
        total = count_msg[0]
        for g in range(1, groups):
            total = total + count_msg[g]
        lines = [counts_ref[...].astype(F32)]
        for s in range(steps):
            lines.append(lines[-1] + total[s : s + 1, :])
        lines.append(jnp.ones((128 - len(lines), lists), F32))
        weight_col[...] = jnp.transpose(jnp.concatenate(lines, axis=0))

    def update(s, last):
        def body(q):
            at = rows_at(q * quarter, quarter)
            after = weight_col[at, s + 1 : s + 2]

            def add(ref):
                value = num[at, :]
                if s == 0:
                    value = value * weight_col[at, 0:1]
                value = value + ref[s, q].astype(F32)
                mean = value * (1.0 / after)
                if last:
                    num[at, :] = mean
                else:
                    num[at, :] = value
                    top = mean.astype(BF16)
                    high[at, :] = top
                    low[at, :] = (mean - top.astype(F32)).astype(BF16)

            @pl.when(q < z)
            def _():
                add(from_left)

            @pl.when(q == z)
            def _():
                add(part)

            @pl.when(q > z)
            def _():
                add(from_right)

        loop(groups, body)

    def to_right(src, s, q):
        return pltpu.make_async_remote_copy(
            src_ref=src.at[s, q], dst_ref=from_left.at[s, q], send_sem=right_send, recv_sem=left_recv.at[s, q],
            device_id={"grp": lax.rem(z + 1, groups)}, device_id_type=MESH,
        )

    def to_left(src, s, q):
        return pltpu.make_async_remote_copy(
            src_ref=src.at[s, q], dst_ref=from_right.at[s, q], send_sem=left_send, recv_sem=right_recv.at[s, q],
            device_id={"grp": lax.rem(z + groups - 1, groups)}, device_id_type=MESH,
        )

    def wait_left(s, q):
        pltpu.make_async_copy(from_left.at[s, q], from_left.at[s, q], left_recv.at[s, q]).wait()

    def wait_right(s, q):
        pltpu.make_async_copy(from_right.at[s, q], from_right.at[s, q], right_recv.at[s, q]).wait()

    def add_into(ref, s, q):
        ref[s, q] = (ref[s, q].astype(F32) + part[s, q].astype(F32)).astype(BF16)

    def reduce_hop(s, t):
        @pl.when(z == t)
        def _():
            for q in range(groups - 1, t, -1):
                if t > 0:
                    wait_left(s, q)
                    add_into(from_left, s, q)
                    to_right(from_left, s, q).start()
                else:
                    to_right(part, s, q).start()

        @pl.when(z == groups - 1 - t)
        def _():
            for q in range(groups - 1 - t):
                if t > 0:
                    wait_right(s, q)
                    add_into(from_right, s, q)
                    to_left(from_right, s, q).start()
                else:
                    to_left(part, s, q).start()

    def total(s):
        @pl.when(z > 0)
        def _():
            wait_left(s, z)

        @pl.when(z < groups - 1)
        def _():
            wait_right(s, z)

        @pl.when(z == 0)
        def _():
            add_into_part(s, (from_right,))

        @pl.when(z == groups - 1)
        def _():
            add_into_part(s, (from_left,))

        @pl.when((z > 0) & (z < groups - 1))
        def _():
            add_into_part(s, (from_left, from_right))

    def add_into_part(s, refs):
        value = part[s, z].astype(F32)
        for ref in refs:
            value = value + ref[s, z].astype(F32)
        part[s, z] = value.astype(BF16)

    def share_own(s):
        @pl.when(z < groups - 1)
        def _():
            to_right(part, s, z).start()

        @pl.when(z > 0)
        def _():
            to_left(part, s, z).start()

    def share_hop(s, t):
        @pl.when(z - t >= 0)
        def _():
            q = z - t
            wait_left(s, q)

            @pl.when(z < groups - 1)
            def _():
                to_right(from_left, s, q).start()

        @pl.when(z + t < groups)
        def _():
            q = z + t
            wait_right(s, q)

            @pl.when(z > 0)
            def _():
                to_left(from_right, s, q).start()

    pack_rows(0)
    exchange(send, recv, 0, disp_send, disp_recv)
    pack_rows(1)
    pack_rows(2)
    get_slots()
    loads[steps].wait()
    split_table()
    drain(recv, 0, disp_recv)
    exchange(send, recv, 1, disp_send, disp_recv)
    list_sums(0)

    def hook(k, t):
        if (k, t) == (0, 0):
            residual(0)
        elif (k, t) == (0, 1):
            drain(recv, 1, disp_recv)
            exchange(send, recv, 2, disp_send, disp_recv)
            list_sums(1)
        elif (k, t) == (1, 0):
            drain(recv, 2, disp_recv)
            list_sums(2)
            send_counts()
        elif (k, t) == (1, 1):
            unpack_rows(0)
            get_counts()
        elif (k, t) == (2, 0):
            update(0, False)
            residual(1)
        elif (k, t) == (3, 0):
            update(1, False)
            residual(2)
        elif (k, t) == (3, 1):
            unpack_rows(1)

    for k in range(steps + 1):
        if k > 0:
            share_own(k - 1)
        for t in range(groups - 1):
            if k < steps:
                reduce_hop(k, t)
            hook(k, t)
            if k > 0:
                share_hop(k - 1, t + 1)
        if k < steps:
            total(k)

    update(steps - 1, True)
    store = pltpu.make_async_copy(num, new_hbm, out_sem.at[steps])
    store.start()
    unpack_rows(2)

    others = send_slots.at[pl.ds(0, owners - 1)]
    pltpu.make_async_copy(others, others, slot_send).wait()
    others = count_msg.at[pl.ds(0, groups - 1)]
    pltpu.make_async_copy(others, others, cnt_send).wait()
    for s in range(steps):
        drain(send, s, disp_send)
        drain(recv, s, ret_send)
        pltpu.make_async_copy(vec.at[s], out_hbm.at[s], out_sem.at[s]).wait()

    @pl.when(z < groups - 1)
    def _():
        pltpu.make_async_copy(from_left, from_left, right_send).wait()

    @pl.when(z > 0)
    def _():
        pltpu.make_async_copy(from_right, from_right, left_send).wait()

    store.wait()


def local(vectors, owner_route, list_slot, centroids, counts):
    steps, rows, width = vectors.shape
    owners = lax.axis_size("list")
    groups = lax.axis_size("grp")
    lists = centroids.shape[0]
    cap = 2 * rows // owners
    places = owners * cap
    quarter = lists // groups
    dims = (steps, rows, width, owners, groups, lists, cap)
    vmem = pl.BlockSpec(memory_space=pltpu.VMEM)
    hbm = pl.BlockSpec(memory_space=pl.ANY)
    dma = pltpu.SemaphoreType.DMA
    return pl.pallas_call(
        functools.partial(kernel, dims),
        out_shape=(
            jax.ShapeDtypeStruct((steps, rows, width), BF16),
            jax.ShapeDtypeStruct((lists, width), F32),
        ),
        in_specs=[hbm, vmem, vmem, hbm, vmem],
        out_specs=(hbm, hbm),
        scratch_shapes=[
            pltpu.VMEM((steps, rows, width), BF16),
            pltpu.VMEM((steps, places, width), BF16),
            pltpu.VMEM((steps, places, width), BF16),
            pltpu.VMEM((steps, places, width), BF16),
            pltpu.VMEM((steps, groups, quarter, width), BF16),
            pltpu.VMEM((steps, groups, quarter, width), BF16),
            pltpu.VMEM((steps, groups, quarter, width), BF16),
            pltpu.VMEM((lists, width), F32),
            pltpu.VMEM((lists, width), BF16),
            pltpu.VMEM((lists, width), BF16),
            pltpu.VMEM((owners, 8, 128), F32),
            pltpu.VMEM((owners, 8, 128), F32),
            pltpu.VMEM((8, places), I32),
            pltpu.VMEM((places, 128), I32),
            pltpu.VMEM((8, rows), I32),
            pltpu.VMEM((rows, 128), I32),
            pltpu.VMEM((lists, 128), F32),
            pltpu.VMEM((groups, 8, lists), F32),
            pltpu.VMEM((lists, 128), F32),
            dma((steps + 1,)),
            dma((steps + 1,)),
            dma,
            dma,
            dma((steps,)),
            dma((steps,)),
            dma((steps,)),
            dma((steps,)),
            dma,
            dma,
            dma((steps, groups)),
            dma((steps, groups)),
            dma,
            dma,
        ],
        compiler_params=pltpu.CompilerParams(
            collective_id=0, has_side_effects=True, vmem_limit_bytes=60 * 1024 * 1024
        ),
        cost_estimate=pl.CostEstimate(flops=30_000_000_000, bytes_accessed=14_000_000, transcendentals=0),
    )(vectors, owner_route[:, :, 0], list_slot, centroids, counts.reshape(1, lists))


def solution(mesh):
    in_specs = (
        P(None, ("grp", "list"), None),
        P(None, ("grp", "list"), None),
        P(None, ("grp", "list")),
        P("list", None),
        P("list"),
    )
    out_specs = (P(None, ("grp", "list"), None), P("list", None))
    return jax.shard_map(local, mesh=mesh, in_specs=in_specs, out_specs=out_specs, check_vma=False)
```

```python
import functools

import jax
import jax.numpy as jnp
from jax import lax
from jax.experimental import pallas as pl
from jax.experimental.pallas import tpu as pltpu
from jax.sharding import PartitionSpec as P

MESH = pl.DeviceIdType.MESH
WIDE = 256
BF16 = jnp.bfloat16
F32 = jnp.float32
I32 = jnp.int32


def one_hot(mask):
    return jnp.where(mask, 1.0, 0.0).astype(BF16)


def dot(a, b):
    return jnp.dot(a, b, preferred_element_type=F32)


def loop(count, body):
    def step(i, carry):
        body(i)
        return carry

    lax.fori_loop(0, count, step, 0)


def cols(c):
    return pl.ds(c * WIDE, WIDE)


def rows_at(start, size):
    return pl.ds(pl.multiple_of(start, size), size)


def kernel(
    dims,
    vec_hbm, owner_ref, slot_ref, cent_hbm, counts_ref,
    out_hbm, new_hbm,
    vec, send, recv, back, part, from_left, from_right, num, high, low, pack_mat, unpack_mat, list_mat, pick_mat,
    send_slots, recv_slots, slot_row, slot_col, dest_row, dest_col, count_col, count_msg, weight_col,
    load_sem, out_sem, slot_send, slot_recv, disp_send, disp_recv, ret_send, ret_recv,
    right_send, left_send, left_recv, right_recv, cnt_send, cnt_recv,
):
    steps, rows, width, owners, groups, lists, cap = dims
    places = owners * cap
    half = lists // 2
    chunks = width // WIDE
    assert groups == 4
    pack = 128 // cap
    me = lax.axis_index("list")
    z = lax.axis_index("grp")

    loads = [pltpu.make_async_copy(vec_hbm.at[s], vec.at[s], load_sem.at[s]) for s in range(steps)]
    for c in range(chunks):
        loads.append(pltpu.make_async_copy(cent_hbm.at[:, cols(c)], num.at[c], load_sem.at[steps + c]))
    for load in loads:
        load.start()

    barrier = pltpu.get_barrier_semaphore()

    def greet_owner(i):
        pl.semaphore_signal(barrier, inc=1, device_id={"list": lax.rem(me + i + 1, owners)}, device_id_type=MESH)

    def greet_group(i):
        pl.semaphore_signal(barrier, inc=1, device_id={"grp": lax.rem(z + i + 1, groups)}, device_id_type=MESH)

    loop(owners - 1, greet_owner)
    loop(groups - 1, greet_group)

    owner_iota = lax.broadcasted_iota(I32, (owners, rows), 0)
    before = one_hot(
        lax.broadcasted_iota(I32, (rows, rows), 0) < lax.broadcasted_iota(I32, (rows, rows), 1)
    )
    hits, ranks, dests = [], [], []
    for s in range(steps):
        hit = jnp.where(owner_iota == owner_ref[s : s + 1, :], 1.0, 0.0)
        rank = hit * dot(hit.astype(BF16), before)
        hits.append(hit)
        ranks.append(jnp.sum(rank, axis=0, keepdims=True))
        dests.append(jnp.sum(rank + hit * (owner_iota * cap).astype(F32), axis=0, keepdims=True))
        dest_row[s : s + 1, :] = dests[s].astype(I32)
    table = jnp.concatenate(dests + ranks + [jnp.zeros((128 - 2 * steps, rows), F32)], axis=0)
    dest_col[...] = jnp.transpose(table).astype(I32)

    send_slots[...] = jnp.zeros_like(send_slots)
    lane = lax.broadcasted_iota(I32, (rows, 128), 1)
    for s in range(steps):
        value = slot_ref[s : s + 1, :] + 1
        upper = (value // 32).astype(F32)
        lower = (value % 32).astype(F32)
        spot = one_hot(lane == dest_col[:, steps + s : steps + s + 1] + lax.rem(me, pack) * cap)
        line = 32.0 * dot((hits[s] * upper).astype(BF16), spot) + dot((hits[s] * lower).astype(BF16), spot)
        for p in range(owners):
            send_slots[p, s : s + 1, :] = line[p : p + 1, :]
    recv_slots[me] = send_slots[me]

    pl.semaphore_wait(barrier, owners - 1 + groups - 1)

    def send_slot(i):
        p = lax.rem(me + i + 1, owners)
        pltpu.make_async_remote_copy(
            src_ref=send_slots.at[p], dst_ref=recv_slots.at[me], send_sem=slot_send, recv_sem=slot_recv,
            device_id={"list": p}, device_id_type=MESH,
        ).start()

    loop(owners - 1, send_slot)

    tile = min(256, places)
    list_tile = min(256, half)
    row_tile = min(256, rows)

    def pack_rows(s, c):
        if c == 0:
            loads[s].wait()
            place = lax.broadcasted_iota(I32, (places, rows), 0)
            pack_mat[...] = one_hot(place == dest_row[s : s + 1, :])

        def body(i):
            at = rows_at(i * tile, tile)
            send[s, c, at, :] = dot(pack_mat[at, :], vec[s, :, cols(c)]).astype(BF16)

        loop(places // tile, body)
        mine = rows_at(me * cap, cap)
        recv[s, c, mine, :] = send[s, c, mine, :]

    def exchange(src, dst, s, c, send_sem, recv_sem):
        def body(i):
            p = lax.rem(me + i + 1, owners)
            pltpu.make_async_remote_copy(
                src_ref=src.at[s, c, rows_at(p * cap, cap)], dst_ref=dst.at[s, c, rows_at(me * cap, cap)],
                send_sem=send_sem.at[s, c], recv_sem=recv_sem.at[s, c],
                device_id={"list": p}, device_id_type=MESH,
            ).start()

        loop(owners - 1, body)

    def dispatch(s, c):
        exchange(send, recv, s, c, disp_send, disp_recv)

    def drain(ref, s, c, sem):
        others = ref.at[s, c, pl.ds(0, (owners - 1) * cap)]
        pltpu.make_async_copy(others, others, sem.at[s, c]).wait()

    def split_table():
        for c in range(chunks):
            loads[steps + c].wait()

        def body(c):
            value = num[c]
            top = value.astype(BF16)
            high[c] = top
            low[c] = (value - top.astype(F32)).astype(BF16)

        loop(chunks, body)

    def get_slots():
        others = recv_slots.at[pl.ds(0, owners - 1)]
        pltpu.make_async_copy(others, others, slot_recv).wait()
        pieces = []
        for c in range(owners // pack):
            piece = recv_slots[c * pack]
            for i in range(1, pack):
                piece = piece + recv_slots[c * pack + i]
            pieces.append(piece)
        line = jnp.concatenate(pieces, axis=1) - 1.0
        slot_row[...] = line.astype(I32)
        tall = jnp.concatenate([line, jnp.zeros((120, places), F32)], axis=0)
        slot_col[...] = jnp.transpose(tall).astype(I32)

    def send_counts():
        count_col[...] = jnp.zeros_like(count_col)

        def body(i):
            at = rows_at(i * list_tile, list_tile)
            name = lax.broadcasted_iota(I32, (list_tile, places), 0) + i * list_tile
            column = lax.broadcasted_iota(I32, (list_tile, 128), 1)
            for s in range(steps):
                found = jnp.sum(jnp.where(name == slot_row[s : s + 1, :], 1.0, 0.0), axis=1, keepdims=True)
                count_col[at, :] = jnp.where(column == s, found, count_col[at, :])

        loop(lists // list_tile, body)
        count_msg[z] = jnp.transpose(count_col[...])[0:8, :]

        def share(i):
            g = lax.rem(z + i + 1, groups)
            pltpu.make_async_remote_copy(
                src_ref=count_msg.at[z], dst_ref=count_msg.at[z], send_sem=cnt_send, recv_sem=cnt_recv,
                device_id={"grp": g}, device_id_type=MESH,
            ).start()

        loop(groups - 1, share)

    def get_counts():
        others = count_msg.at[pl.ds(0, groups - 1)]
        pltpu.make_async_copy(others, others, cnt_recv).wait()
        total = count_msg[0]
        for g in range(1, groups):
            total = total + count_msg[g]
        lines = [counts_ref[...].astype(F32)]
        for s in range(steps):
            lines.append(lines[-1] + total[s : s + 1, :])
        lines.append(jnp.ones((128 - len(lines), lists), F32))
        weight_col[...] = jnp.transpose(jnp.concatenate(lines, axis=0))

    def list_sums(s, c):
        if c == 0:
            name = lax.broadcasted_iota(I32, (lists, places), 0)
            list_mat[...] = one_hot(name == slot_row[s : s + 1, :])
        first = (s * chunks + c) * 2
        for h in range(2):
            def body(i):
                at = rows_at(h * half + i * list_tile, list_tile)
                value = dot(list_mat[at, :], recv[s, c]).astype(BF16)
                to = rows_at(i * list_tile, list_tile)
                part[first, h, to, :] = value[:, :128]
                part[first + 1, h, to, :] = value[:, 128:]

            loop(half // list_tile, body)

    def residual(s, c):
        if c == 0:
            name = lax.broadcasted_iota(I32, (places, lists), 1)
            pick_mat[...] = one_hot(name == slot_col[:, s : s + 1])

        def body(i):
            at = rows_at(i * tile, tile)
            chosen = dot(pick_mat[at, :], high[c]) + dot(pick_mat[at, :], low[c])
            recv[s, c, at, :] = (recv[s, c, at, :].astype(F32) - chosen).astype(BF16)

        loop(places // tile, body)
        mine = rows_at(me * cap, cap)
        back[s, c, mine, :] = recv[s, c, mine, :]
        exchange(recv, back, s, c, ret_send, ret_recv)

    def out_copy(s, c):
        return pltpu.make_async_copy(vec.at[s, :, cols(c)], out_hbm.at[s, :, cols(c)], out_sem.at[s, c])

    def unpack_rows(s, c):
        if c == 0:
            name = lax.broadcasted_iota(I32, (rows, places), 1)
            unpack_mat[...] = one_hot(name == dest_col[:, s : s + 1])
        drain(back, s, c, ret_recv)

        def body(i):
            at = rows_at(i * row_tile, row_tile)
            vec[s, at, cols(c)] = dot(unpack_mat[at, :], back[s, c]).astype(BF16)

        loop(rows // row_tile, body)
        out_copy(s, c).start()

    def new_copy(c):
        return pltpu.make_async_copy(num.at[c], new_hbm.at[:, cols(c)], out_sem.at[steps, c])

    def wait_left(j, h):
        pltpu.make_async_copy(from_left.at[j, h], from_left.at[j, h], left_recv.at[j, h]).wait()

    def wait_right(j, h):
        pltpu.make_async_copy(from_right.at[j, h], from_right.at[j, h], right_recv.at[j, h]).wait()

    def to_right(src, j, h):
        pltpu.make_async_remote_copy(
            src_ref=src.at[j, h], dst_ref=from_left.at[j, h], send_sem=right_send, recv_sem=left_recv.at[j, h],
            device_id={"grp": lax.rem(z + 1, groups)}, device_id_type=MESH,
        ).start()

    def to_left(src, j, h):
        pltpu.make_async_remote_copy(
            src_ref=src.at[j, h], dst_ref=from_right.at[j, h], send_sem=left_send, recv_sem=right_recv.at[j, h],
            device_id={"grp": lax.rem(z + groups - 1, groups)}, device_id_type=MESH,
        ).start()

    def update(s, c):
        first = (s * chunks + c) * 2
        last = s == steps - 1

        @pl.when(z == 0)
        def _():
            for i in range(2):
                wait_right(first + i, 0)
                wait_right(first + i, 1)

        @pl.when(z == groups - 1)
        def _():
            for i in range(2):
                wait_left(first + i, 0)
                wait_left(first + i, 1)

        def add(h, ref):
            def body(i):
                at = rows_at(h * half + i * list_tile, list_tile)
                of = rows_at(i * list_tile, list_tile)
                over = 1.0 / weight_col[at, s + 1 : s + 2]
                sums = jnp.concatenate([ref[first, h, of, :], ref[first + 1, h, of, :]], axis=1)
                value = num[c, at, :]
                if s == 0:
                    value = value * weight_col[at, 0:1]
                value = value + sums.astype(F32)
                mean = value * over
                if last:
                    num[c, at, :] = mean
                else:
                    num[c, at, :] = value
                    top = mean.astype(BF16)
                    high[c, at, :] = top
                    low[c, at, :] = (mean - top.astype(F32)).astype(BF16)

            loop(half // list_tile, body)

        for h in range(2):
            pl.when(z < 1 + h)(functools.partial(add, h, from_right))
            pl.when(z == 1 + h)(functools.partial(add, h, part))
            pl.when(z > 1 + h)(functools.partial(add, h, from_left))
        if last:
            new_copy(c).start()

    pairs = 2 * steps * chunks

    def relay(t):
        def at_lag(lag, who, body):
            @pl.when((z == who) & (t - lag >= 0) & (t - lag < pairs))
            def _():
                body(t - lag)

        def left_end(j):
            to_right(part, j, 1)
            to_right(part, j, 0)

        def right_end(j):
            to_left(part, j, 0)
            to_left(part, j, 1)

        def pass_right(j):
            wait_left(j, 1)
            from_left[j, 1] = (from_left[j, 1].astype(F32) + part[j, 1].astype(F32)).astype(BF16)
            to_right(from_left, j, 1)

        def pass_left(j):
            wait_right(j, 0)
            from_right[j, 0] = (from_right[j, 0].astype(F32) + part[j, 0].astype(F32)).astype(BF16)
            to_left(from_right, j, 0)

        def total(h, j):
            wait_left(j, h)
            wait_right(j, h)
            value = part[j, h].astype(F32) + from_left[j, h].astype(F32) + from_right[j, h].astype(F32)
            part[j, h] = value.astype(BF16)
            to_right(part, j, h)
            to_left(part, j, h)

        def forward_left(j):
            wait_right(j, 1)
            to_left(from_right, j, 1)

        def forward_right(j):
            wait_left(j, 0)
            to_right(from_left, j, 0)

        at_lag(0, 0, left_end)
        at_lag(0, 3, right_end)
        at_lag(1, 1, pass_right)
        at_lag(1, 2, pass_left)
        at_lag(2, 1, functools.partial(total, 0))
        at_lag(2, 2, functools.partial(total, 1))
        at_lag(3, 1, forward_left)
        at_lag(3, 2, forward_right)

    ready, after = {}, {}

    def plan(table, turn, *tasks):
        table.setdefault(turn, []).extend(tasks)

    call = functools.partial
    for c in range(chunks):
        if c + 2 < chunks:
            plan(ready, c, call(drain, recv, 0, c, disp_recv), call(dispatch, 0, c + 2))
        else:
            plan(ready, c, call(drain, recv, 0, c, disp_recv))
        plan(ready, c, call(list_sums, 0, c))
        for s in range(1, steps):
            plan(ready, s * chunks + c, call(drain, recv, s, c, disp_recv), call(list_sums, s, c))
    plan(after, 0, *[call(pack_rows, 1, c) for c in range(chunks)], send_counts, split_table)
    plan(after, 3, get_counts)
    for c in range(chunks):
        plan(after, c, call(residual, 0, c))
        if c == chunks - 2:
            for d in range(chunks):
                plan(after, c, call(dispatch, 1, d))
        if c == chunks - 1:
            plan(after, c, *[call(pack_rows, 2, d) for d in range(chunks)])
    for c in range(chunks):
        plan(after, chunks + c, call(dispatch, 2, c))
    for s in range(steps):
        for c in range(chunks):
            plan(after, s * chunks + c + 3, call(update, s, c))
            if s + 1 < steps:
                plan(after, max((s + 1) * chunks + c, s * chunks + c + 3), call(residual, s + 1, c))
                plan(after, (s + 1) * chunks + c + 1, call(unpack_rows, s, c))

    pack_rows(0, 0)
    dispatch(0, 0)
    pack_rows(0, 1)
    dispatch(0, 1)
    for c in range(2, chunks):
        pack_rows(0, c)
    get_slots()

    for turn in range(steps * chunks + 3):
        for task in ready.get(turn, []):
            task()
        if turn < steps * chunks + 2:
            relay(2 * turn)
            relay(2 * turn + 1)
        for task in after.get(turn, []):
            task()
    for c in range(chunks):
        unpack_rows(steps - 1, c)

    others = send_slots.at[pl.ds(0, owners - 1)]
    pltpu.make_async_copy(others, others, slot_send).wait()
    others = count_msg.at[pl.ds(0, groups - 1)]
    pltpu.make_async_copy(others, others, cnt_send).wait()
    for s in range(steps):
        for c in range(chunks):
            drain(send, s, c, disp_send)
            drain(recv, s, c, ret_send)
            out_copy(s, c).wait()

    @pl.when(z < groups - 1)
    def _():
        pltpu.make_async_copy(from_left, from_left, right_send).wait()

    @pl.when(z > 0)
    def _():
        pltpu.make_async_copy(from_right, from_right, left_send).wait()

    for c in range(chunks):
        new_copy(c).wait()


def local(vectors, owner_route, list_slot, centroids, counts):
    steps, rows, width = vectors.shape
    owners = lax.axis_size("list")
    groups = lax.axis_size("grp")
    lists = centroids.shape[0]
    cap = 2 * rows // owners
    places = owners * cap
    half = lists // 2
    chunks = width // WIDE
    pairs = 2 * steps * chunks
    dims = (steps, rows, width, owners, groups, lists, cap)
    vmem = pl.BlockSpec(memory_space=pltpu.VMEM)
    hbm = pl.BlockSpec(memory_space=pl.ANY)
    dma = pltpu.SemaphoreType.DMA
    return pl.pallas_call(
        functools.partial(kernel, dims),
        out_shape=(
            jax.ShapeDtypeStruct((steps, rows, width), BF16),
            jax.ShapeDtypeStruct((lists, width), F32),
        ),
        in_specs=[hbm, vmem, vmem, hbm, vmem],
        out_specs=(hbm, hbm),
        scratch_shapes=[
            pltpu.VMEM((steps, rows, width), BF16),
            pltpu.VMEM((steps, chunks, places, WIDE), BF16),
            pltpu.VMEM((steps, chunks, places, WIDE), BF16),
            pltpu.VMEM((steps, chunks, places, WIDE), BF16),
            pltpu.VMEM((pairs, 2, half, 128), BF16),
            pltpu.VMEM((pairs, 2, half, 128), BF16),
            pltpu.VMEM((pairs, 2, half, 128), BF16),
            pltpu.VMEM((chunks, lists, WIDE), F32),
            pltpu.VMEM((chunks, lists, WIDE), BF16),
            pltpu.VMEM((chunks, lists, WIDE), BF16),
            pltpu.VMEM((places, rows), BF16),
            pltpu.VMEM((rows, places), BF16),
            pltpu.VMEM((lists, places), BF16),
            pltpu.VMEM((places, lists), BF16),
            pltpu.VMEM((owners, 8, 128), F32),
            pltpu.VMEM((owners, 8, 128), F32),
            pltpu.VMEM((8, places), I32),
            pltpu.VMEM((places, 128), I32),
            pltpu.VMEM((8, rows), I32),
            pltpu.VMEM((rows, 128), I32),
            pltpu.VMEM((lists, 128), F32),
            pltpu.VMEM((groups, 8, lists), F32),
            pltpu.VMEM((lists, 128), F32),
            dma((steps + chunks,)),
            dma((steps + 1, chunks)),
            dma,
            dma,
            dma((steps, chunks)),
            dma((steps, chunks)),
            dma((steps, chunks)),
            dma((steps, chunks)),
            dma,
            dma,
            dma((pairs, 2)),
            dma((pairs, 2)),
            dma,
            dma,
        ],
        compiler_params=pltpu.CompilerParams(
            collective_id=0, has_side_effects=True, vmem_limit_bytes=62 * 1024 * 1024
        ),
        cost_estimate=pl.CostEstimate(flops=30_000_000_000, bytes_accessed=14_000_000, transcendentals=0),
    )(vectors, owner_route[:, :, 0], list_slot, centroids, counts.reshape(1, lists))


def solution(mesh):
    in_specs = (
        P(None, ("grp", "list"), None),
        P(None, ("grp", "list"), None),
        P(None, ("grp", "list")),
        P("list", None),
        P("list"),
    )
    out_specs = (P(None, ("grp", "list"), None), P("list", None))
    return jax.shard_map(local, mesh=mesh, in_specs=in_specs, out_specs=out_specs, check_vma=False)
```

```python
import functools

import jax
import jax.numpy as jnp
from jax import lax
from jax.experimental import pallas as pl
from jax.experimental.pallas import tpu as pltpu
from jax.sharding import PartitionSpec as P

MESH = pl.DeviceIdType.MESH
WIDE = 256
BF16 = jnp.bfloat16
F32 = jnp.float32
I32 = jnp.int32


def one_hot(mask):
    return jnp.where(mask, 1.0, 0.0).astype(BF16)


def dot(a, b):
    return jnp.dot(a, b, preferred_element_type=F32)


def loop(count, body):
    def step(i, carry):
        body(i)
        return carry

    lax.fori_loop(0, count, step, 0)


def cols(c):
    return pl.ds(c * WIDE, WIDE)


def rows_at(start, size):
    return pl.ds(pl.multiple_of(start, size), size)


def kernel(
    dims,
    vec_hbm, owner_ref, slot_ref, cent_hbm, counts_ref,
    out_hbm, new_hbm,
    vec, send, recv, back, part, from_left, from_right, num, high, low, pack_mat, unpack_mat, list_mat, pick_mat,
    send_slots, recv_slots, slot_row, slot_col, dest_row, dest_col, count_col, count_msg, weight_col,
    load_sem, out_sem, slot_send, slot_recv, disp_send, disp_recv, ret_send, ret_recv,
    right_send, left_send, left_recv, right_recv, cnt_send, cnt_recv,
):
    steps, rows, width, owners, groups, lists, cap = dims
    places = owners * cap
    half = lists // 2
    chunks = width // WIDE
    assert groups == 4
    pack = 128 // cap
    me = lax.axis_index("list")
    z = lax.axis_index("grp")

    loads = [pltpu.make_async_copy(vec_hbm.at[s], vec.at[s], load_sem.at[s]) for s in range(steps)]
    for c in range(chunks):
        loads.append(pltpu.make_async_copy(cent_hbm.at[:, cols(c)], num.at[c], load_sem.at[steps + c]))
    for load in loads:
        load.start()

    barrier = pltpu.get_barrier_semaphore()

    def greet_owner(i):
        pl.semaphore_signal(barrier, inc=1, device_id={"list": lax.rem(me + i + 1, owners)}, device_id_type=MESH)

    def greet_group(i):
        pl.semaphore_signal(barrier, inc=1, device_id={"grp": lax.rem(z + i + 1, groups)}, device_id_type=MESH)

    loop(owners - 1, greet_owner)
    loop(groups - 1, greet_group)

    owner_iota = lax.broadcasted_iota(I32, (owners, rows), 0)
    before = one_hot(
        lax.broadcasted_iota(I32, (rows, rows), 0) < lax.broadcasted_iota(I32, (rows, rows), 1)
    )
    hits, ranks, dests = [], [], []
    for s in range(steps):
        hit = jnp.where(owner_iota == owner_ref[s : s + 1, :], 1.0, 0.0)
        rank = hit * dot(hit.astype(BF16), before)
        hits.append(hit)
        ranks.append(jnp.sum(rank, axis=0, keepdims=True))
        dests.append(jnp.sum(rank + hit * (owner_iota * cap).astype(F32), axis=0, keepdims=True))
        dest_row[s : s + 1, :] = dests[s].astype(I32)
    table = jnp.concatenate(dests + ranks + [jnp.zeros((128 - 2 * steps, rows), F32)], axis=0)
    dest_col[...] = jnp.transpose(table).astype(I32)

    send_slots[...] = jnp.zeros_like(send_slots)
    lane = lax.broadcasted_iota(I32, (rows, 128), 1)
    for s in range(steps):
        value = slot_ref[s : s + 1, :] + 1
        upper = (value // 32).astype(F32)
        lower = (value % 32).astype(F32)
        spot = one_hot(lane == dest_col[:, steps + s : steps + s + 1] + lax.rem(me, pack) * cap)
        line = 32.0 * dot((hits[s] * upper).astype(BF16), spot) + dot((hits[s] * lower).astype(BF16), spot)
        for p in range(owners):
            send_slots[p, s : s + 1, :] = line[p : p + 1, :]
    recv_slots[me] = send_slots[me]

    pl.semaphore_wait(barrier, owners - 1 + groups - 1)

    def send_slot(i):
        p = lax.rem(me + i + 1, owners)
        pltpu.make_async_remote_copy(
            src_ref=send_slots.at[p], dst_ref=recv_slots.at[me], send_sem=slot_send, recv_sem=slot_recv,
            device_id={"list": p}, device_id_type=MESH,
        ).start()

    loop(owners - 1, send_slot)

    tile = min(256, places)
    list_tile = min(256, half)
    row_tile = min(256, rows)

    def pack_rows(s, c):
        if c == 0:
            loads[s].wait()
            place = lax.broadcasted_iota(I32, (places, rows), 0)
            pack_mat[...] = one_hot(place == dest_row[s : s + 1, :])

        def body(i):
            at = rows_at(i * tile, tile)
            send[s, c, at, :] = dot(pack_mat[at, :], vec[s, :, cols(c)]).astype(BF16)

        loop(places // tile, body)
        mine = rows_at(me * cap, cap)
        recv[s, c, mine, :] = send[s, c, mine, :]

    def exchange(src, dst, s, c, send_sem, recv_sem):
        def body(i):
            p = lax.rem(me + i + 1, owners)
            pltpu.make_async_remote_copy(
                src_ref=src.at[s, c, rows_at(p * cap, cap)], dst_ref=dst.at[s, c, rows_at(me * cap, cap)],
                send_sem=send_sem.at[s, c], recv_sem=recv_sem.at[s, c],
                device_id={"list": p}, device_id_type=MESH,
            ).start()

        loop(owners - 1, body)

    def dispatch(s, c):
        exchange(send, recv, s, c, disp_send, disp_recv)

    def drain(ref, s, c, sem):
        others = ref.at[s, c, pl.ds(0, (owners - 1) * cap)]
        pltpu.make_async_copy(others, others, sem.at[s, c]).wait()

    def split_table(c):
        loads[steps + c].wait()

        def body(i):
            at = rows_at(i * list_tile, list_tile)
            value = num[c, at, :]
            top = value.astype(BF16)
            high[c, at, :] = top
            low[c, at, :] = (value - top.astype(F32)).astype(BF16)

        loop(lists // list_tile, body)

    def get_slots():
        others = recv_slots.at[pl.ds(0, owners - 1)]
        pltpu.make_async_copy(others, others, slot_recv).wait()
        pieces = []
        for c in range(owners // pack):
            piece = recv_slots[c * pack]
            for i in range(1, pack):
                piece = piece + recv_slots[c * pack + i]
            pieces.append(piece)
        line = jnp.concatenate(pieces, axis=1) - 1.0
        slot_row[...] = line.astype(I32)
        tall = jnp.concatenate([line, jnp.zeros((120, places), F32)], axis=0)
        slot_col[...] = jnp.transpose(tall).astype(I32)

    def send_counts():
        count_col[...] = jnp.zeros_like(count_col)

        def body(i):
            at = rows_at(i * list_tile, list_tile)
            name = lax.broadcasted_iota(I32, (list_tile, places), 0) + i * list_tile
            column = lax.broadcasted_iota(I32, (list_tile, 128), 1)
            for s in range(steps):
                found = jnp.sum(jnp.where(name == slot_row[s : s + 1, :], 1.0, 0.0), axis=1, keepdims=True)
                count_col[at, :] = jnp.where(column == s, found, count_col[at, :])

        loop(lists // list_tile, body)
        count_msg[z] = jnp.transpose(count_col[...])[0:8, :]

        def share(i):
            g = lax.rem(z + i + 1, groups)
            pltpu.make_async_remote_copy(
                src_ref=count_msg.at[z], dst_ref=count_msg.at[z], send_sem=cnt_send, recv_sem=cnt_recv,
                device_id={"grp": g}, device_id_type=MESH,
            ).start()

        loop(groups - 1, share)

    def get_counts():
        others = count_msg.at[pl.ds(0, groups - 1)]
        pltpu.make_async_copy(others, others, cnt_recv).wait()
        total = count_msg[0]
        for g in range(1, groups):
            total = total + count_msg[g]
        lines = [counts_ref[...].astype(F32)]
        for s in range(steps):
            lines.append(lines[-1] + total[s : s + 1, :])
        lines.append(jnp.ones((128 - len(lines), lists), F32))
        weight_col[...] = jnp.transpose(jnp.concatenate(lines, axis=0))

    def list_sums(s, c):
        if c == 0:
            name = lax.broadcasted_iota(I32, (lists, places), 0)
            list_mat[...] = one_hot(name == slot_row[s : s + 1, :])
        first = (s * chunks + c) * 2
        for h in range(2):
            def body(i):
                at = rows_at(h * half + i * list_tile, list_tile)
                value = dot(list_mat[at, :], recv[s, c]).astype(BF16)
                to = rows_at(i * list_tile, list_tile)
                part[first, h, to, :] = value[:, :128]
                part[first + 1, h, to, :] = value[:, 128:]

            loop(half // list_tile, body)

    def residual(s, c):
        if c == 0:
            name = lax.broadcasted_iota(I32, (places, lists), 1)
            pick_mat[...] = one_hot(name == slot_col[:, s : s + 1])

        def body(i):
            at = rows_at(i * tile, tile)
            chosen = dot(pick_mat[at, :], high[c]) + dot(pick_mat[at, :], low[c])
            recv[s, c, at, :] = (recv[s, c, at, :].astype(F32) - chosen).astype(BF16)

        loop(places // tile, body)
        mine = rows_at(me * cap, cap)
        back[s, c, mine, :] = recv[s, c, mine, :]
        exchange(recv, back, s, c, ret_send, ret_recv)

    def out_copy(s, c):
        return pltpu.make_async_copy(vec.at[s, :, cols(c)], out_hbm.at[s, :, cols(c)], out_sem.at[s, c])

    def unpack_rows(s, c):
        if c == 0:
            name = lax.broadcasted_iota(I32, (rows, places), 1)
            unpack_mat[...] = one_hot(name == dest_col[:, s : s + 1])
        drain(back, s, c, ret_recv)

        def body(i):
            at = rows_at(i * row_tile, row_tile)
            vec[s, at, cols(c)] = dot(unpack_mat[at, :], back[s, c]).astype(BF16)

        loop(rows // row_tile, body)
        out_copy(s, c).start()

    def new_copy(c):
        return pltpu.make_async_copy(num.at[c], new_hbm.at[:, cols(c)], out_sem.at[steps, c])

    def wait_left(j, h):
        pltpu.make_async_copy(from_left.at[j, h], from_left.at[j, h], left_recv.at[j, h]).wait()

    def wait_right(j, h):
        pltpu.make_async_copy(from_right.at[j, h], from_right.at[j, h], right_recv.at[j, h]).wait()

    def to_right(src, j, h):
        pltpu.make_async_remote_copy(
            src_ref=src.at[j, h], dst_ref=from_left.at[j, h], send_sem=right_send, recv_sem=left_recv.at[j, h],
            device_id={"grp": lax.rem(z + 1, groups)}, device_id_type=MESH,
        ).start()

    def to_left(src, j, h):
        pltpu.make_async_remote_copy(
            src_ref=src.at[j, h], dst_ref=from_right.at[j, h], send_sem=left_send, recv_sem=right_recv.at[j, h],
            device_id={"grp": lax.rem(z + groups - 1, groups)}, device_id_type=MESH,
        ).start()

    def update(s, c):
        first = (s * chunks + c) * 2
        last = s == steps - 1

        @pl.when(z == 0)
        def _():
            for i in range(2):
                wait_right(first + i, 0)
                wait_right(first + i, 1)

        @pl.when(z == groups - 1)
        def _():
            for i in range(2):
                wait_left(first + i, 0)
                wait_left(first + i, 1)

        def add(h, ref):
            def body(i):
                at = rows_at(h * half + i * list_tile, list_tile)
                of = rows_at(i * list_tile, list_tile)
                over = 1.0 / weight_col[at, s + 1 : s + 2]
                sums = jnp.concatenate([ref[first, h, of, :], ref[first + 1, h, of, :]], axis=1)
                value = num[c, at, :]
                if s == 0:
                    value = value * weight_col[at, 0:1]
                value = value + sums.astype(F32)
                mean = value * over
                if last:
                    num[c, at, :] = mean
                else:
                    num[c, at, :] = value
                    top = mean.astype(BF16)
                    high[c, at, :] = top
                    low[c, at, :] = (mean - top.astype(F32)).astype(BF16)

            loop(half // list_tile, body)

        for h in range(2):
            pl.when(z < 1 + h)(functools.partial(add, h, from_right))
            pl.when(z == 1 + h)(functools.partial(add, h, part))
            pl.when(z > 1 + h)(functools.partial(add, h, from_left))
        if last:
            new_copy(c).start()

    pairs = 2 * steps * chunks

    def relay(t):
        def at_lag(lag, who, body):
            @pl.when((z == who) & (t - lag >= 0) & (t - lag < pairs))
            def _():
                body(t - lag)

        def left_end(j):
            to_right(part, j, 1)
            to_right(part, j, 0)

        def right_end(j):
            to_left(part, j, 0)
            to_left(part, j, 1)

        def pass_right(j):
            wait_left(j, 1)
            from_left[j, 1] = (from_left[j, 1].astype(F32) + part[j, 1].astype(F32)).astype(BF16)
            to_right(from_left, j, 1)

        def pass_left(j):
            wait_right(j, 0)
            from_right[j, 0] = (from_right[j, 0].astype(F32) + part[j, 0].astype(F32)).astype(BF16)
            to_left(from_right, j, 0)

        def total(h, j):
            wait_left(j, h)
            wait_right(j, h)
            value = part[j, h].astype(F32) + from_left[j, h].astype(F32) + from_right[j, h].astype(F32)
            part[j, h] = value.astype(BF16)
            to_right(part, j, h)
            to_left(part, j, h)

        def forward_left(j):
            wait_right(j, 1)
            to_left(from_right, j, 1)

        def forward_right(j):
            wait_left(j, 0)
            to_right(from_left, j, 0)

        at_lag(0, 0, left_end)
        at_lag(0, 3, right_end)
        at_lag(1, 1, pass_right)
        at_lag(1, 2, pass_left)
        at_lag(2, 1, functools.partial(total, 0))
        at_lag(2, 2, functools.partial(total, 1))
        at_lag(3, 1, forward_left)
        at_lag(3, 2, forward_right)

    ready, after = {}, {}

    def plan(table, turn, *tasks):
        table.setdefault(turn, []).extend(tasks)

    call = functools.partial
    for c in range(chunks):
        if c + 2 < chunks:
            plan(ready, c, call(drain, recv, 0, c, disp_recv), call(dispatch, 0, c + 2))
        else:
            plan(ready, c, call(drain, recv, 0, c, disp_recv))
        plan(ready, c, call(list_sums, 0, c))
        for s in range(1, steps):
            plan(ready, s * chunks + c, call(drain, recv, s, c, disp_recv), call(list_sums, s, c))
    plan(after, 1, send_counts)
    plan(after, 3, get_counts)
    for c in range(chunks):
        turn = min(max(c, 1), chunks - 1)
        plan(after, turn, call(pack_rows, 1, c), call(dispatch, 1, c))
        plan(after, c + 1, call(split_table, c), call(residual, 0, c))
        plan(after, chunks + c, call(pack_rows, 2, c), call(dispatch, 2, c))
    for s in range(steps):
        for c in range(chunks):
            plan(after, s * chunks + c + 3, call(update, s, c))
            if s + 1 < steps:
                plan(after, max((s + 1) * chunks + c, s * chunks + c + 3), call(residual, s + 1, c))
            plan(after, min(s * chunks + c + 3, steps * chunks + 1), call(unpack_rows, s, c))

    pack_rows(0, 0)
    dispatch(0, 0)
    pack_rows(0, 1)
    dispatch(0, 1)
    for c in range(2, chunks):
        pack_rows(0, c)
    get_slots()

    for turn in range(steps * chunks + 3):
        for task in ready.get(turn, []):
            task()
        tasks = after.get(turn, [])
        middle = len(tasks) // 2
        relays = turn < steps * chunks + 2
        if relays:
            relay(2 * turn)
        for task in tasks[:middle]:
            task()
        if relays:
            relay(2 * turn + 1)
        for task in tasks[middle:]:
            task()

    others = send_slots.at[pl.ds(0, owners - 1)]
    pltpu.make_async_copy(others, others, slot_send).wait()
    others = count_msg.at[pl.ds(0, groups - 1)]
    pltpu.make_async_copy(others, others, cnt_send).wait()
    for s in range(steps):
        for c in range(chunks):
            drain(send, s, c, disp_send)
            drain(recv, s, c, ret_send)
            out_copy(s, c).wait()

    @pl.when(z < groups - 1)
    def _():
        pltpu.make_async_copy(from_left, from_left, right_send).wait()

    @pl.when(z > 0)
    def _():
        pltpu.make_async_copy(from_right, from_right, left_send).wait()

    for c in range(chunks):
        new_copy(c).wait()


def local(vectors, owner_route, list_slot, centroids, counts):
    steps, rows, width = vectors.shape
    owners = lax.axis_size("list")
    groups = lax.axis_size("grp")
    lists = centroids.shape[0]
    cap = 2 * rows // owners
    places = owners * cap
    half = lists // 2
    chunks = width // WIDE
    pairs = 2 * steps * chunks
    dims = (steps, rows, width, owners, groups, lists, cap)
    vmem = pl.BlockSpec(memory_space=pltpu.VMEM)
    hbm = pl.BlockSpec(memory_space=pl.ANY)
    dma = pltpu.SemaphoreType.DMA
    return pl.pallas_call(
        functools.partial(kernel, dims),
        out_shape=(
            jax.ShapeDtypeStruct((steps, rows, width), BF16),
            jax.ShapeDtypeStruct((lists, width), F32),
        ),
        in_specs=[hbm, vmem, vmem, hbm, vmem],
        out_specs=(hbm, hbm),
        scratch_shapes=[
            pltpu.VMEM((steps, rows, width), BF16),
            pltpu.VMEM((steps, chunks, places, WIDE), BF16),
            pltpu.VMEM((steps, chunks, places, WIDE), BF16),
            pltpu.VMEM((steps, chunks, places, WIDE), BF16),
            pltpu.VMEM((pairs, 2, half, 128), BF16),
            pltpu.VMEM((pairs, 2, half, 128), BF16),
            pltpu.VMEM((pairs, 2, half, 128), BF16),
            pltpu.VMEM((chunks, lists, WIDE), F32),
            pltpu.VMEM((chunks, lists, WIDE), BF16),
            pltpu.VMEM((chunks, lists, WIDE), BF16),
            pltpu.VMEM((places, rows), BF16),
            pltpu.VMEM((rows, places), BF16),
            pltpu.VMEM((lists, places), BF16),
            pltpu.VMEM((places, lists), BF16),
            pltpu.VMEM((owners, 8, 128), F32),
            pltpu.VMEM((owners, 8, 128), F32),
            pltpu.VMEM((8, places), I32),
            pltpu.VMEM((places, 128), I32),
            pltpu.VMEM((8, rows), I32),
            pltpu.VMEM((rows, 128), I32),
            pltpu.VMEM((lists, 128), F32),
            pltpu.VMEM((groups, 8, lists), F32),
            pltpu.VMEM((lists, 128), F32),
            dma((steps + chunks,)),
            dma((steps + 1, chunks)),
            dma,
            dma,
            dma((steps, chunks)),
            dma((steps, chunks)),
            dma((steps, chunks)),
            dma((steps, chunks)),
            dma,
            dma,
            dma((pairs, 2)),
            dma((pairs, 2)),
            dma,
            dma,
        ],
        compiler_params=pltpu.CompilerParams(
            collective_id=0, has_side_effects=True, vmem_limit_bytes=62 * 1024 * 1024
        ),
        cost_estimate=pl.CostEstimate(flops=30_000_000_000, bytes_accessed=14_000_000, transcendentals=0),
    )(vectors, owner_route[:, :, 0], list_slot, centroids, counts.reshape(1, lists))


def solution(mesh):
    in_specs = (
        P(None, ("grp", "list"), None),
        P(None, ("grp", "list"), None),
        P(None, ("grp", "list")),
        P("list", None),
        P("list"),
    )
    out_specs = (P(None, ("grp", "list"), None), P("list", None))
    return jax.shard_map(local, mesh=mesh, in_specs=in_specs, out_specs=out_specs, check_vma=False)
```
